32 devices in a mesh: leaf: 8 (over z, x), row: 4 (over y, core).
Axes of the slice: x: 2, y: 2, z: 4, core: 2. Of those that a mesh axis runs over, the one named last changes fastest.
Arguments:
- sec_rhs: float32 [64, 4096], P(None, ('leaf', 'row')), may hold values from -6 to 6
- sec_inverse: float32 [4096, 512], P(('leaf', 'row')), as said below
- sep_rhs: float32 [4, 64, 1024], P(None, None, 'leaf'), may hold values from -6 to 6
- sep_inverse: float32 [4, 1024, 1024], P(None, 'leaf'), as said below
- sep_coupling: float32 [3, 1024, 1024], P(None, 'leaf'), may hold values from -0.1875 to 0.1875
- sec_update: float32 [4, 1024, 4096], P(None, None, ('leaf', 'row')), may hold values from -0.1875 to 0.1875
- link: int32 [8, 4], P('leaf'), may hold values 0 or 1
Outputs:
- sec_solution: float32 [64, 4096], P(None, ('leaf', 'row'))
- sep_solution: float32 [4, 64, 1024], P(None, None, 'leaf')
The draws below stay inside these ranges and needn't reach their ends.
Inputs may be any that keep to these rules, and one draw needn't show every extreme that they name: link holds only 0 and 1. Each section's block of sec_inverse is lower triangular with entries on the diagonal between 0.7 and 1.3. Each block of sep_inverse is lower triangular with entries on the diagonal between 0.7 and 1.3.
All inputs are finite; a program needn't handle non-finite values. No bound on the sum of `link` on one device may be relied on, other than what follows from the above.
Results may differ from the reference program's by a relative error of at most 0.00013.
Values sent between devices are 32-bit elements; how exact they have to be, the bound alone decides.
A program may use at most 128 MiB of HBM per device.

```python
import math
import jax
import jax.numpy as jnp
from jax import lax

RHS = 64
LEVELS = 4
SECTIONS = 8
NS = 512
NK = 1024


def lower_inverse(key, shape, order, row_axis):
    key_off, key_diag = jax.random.split(key)
    spread = 0.6 / math.sqrt(order)
    off_part = jax.random.normal(key_off, shape, jnp.float32) * spread
    diag_part = jax.random.uniform(key_diag, shape, jnp.float32, 0.8, 1.2)
    rows_index = lax.broadcasted_iota(jnp.int32, shape, row_axis) % order
    cols_index = lax.broadcasted_iota(jnp.int32, shape, len(shape) - 1)
    lower = jnp.where(cols_index < rows_index, off_part, 0.0)
    return lower + jnp.where(cols_index == rows_index, diag_part, 0.0)


def draw_sec_inverse(key, part):
    return lower_inverse(jax.random.fold_in(key, 11), (NS * SECTIONS, NS), NS, 0)


def draw_sep_inverse(key, part):
    return lower_inverse(jax.random.fold_in(key, 23), (LEVELS, NK, NK), NK, 1)


def place_ends(result, key, smallest, top_value):
    place = [jax.random.randint(jax.random.fold_in(key, axis), (), 0, length) for axis, length in enumerate(result.shape)]
    widest = result.shape.index(max(result.shape))
    neighbour = place[:widest] + [(place[widest] + 1) % result.shape[widest]] + place[widest + 1:]
    return result.at[tuple(place)].set(smallest).at[tuple(neighbour)].set(top_value)


def with_spikes(drawn, stream_key, source, target, shards_of, factor):
    def block_of(dim):
        return (jnp.arange(drawn.shape[dim]) // (drawn.shape[dim] // shards_of)).reshape((-1,) + (1,) * (drawn.ndim - 1 - dim))

    one_side = jax.random.permutation(stream_key, shards_of)[block_of(target)]
    other_side = (block_of(target) + shards_of // 2) % shards_of
    return jnp.where((block_of(source) == one_side) | (block_of(source) == other_side), factor * drawn, drawn)


def shard_levels(key, extent, pieces, smallest, top_value):
    gain, own = 1.0, jax.random.fold_in(key, 6)
    for position, shards_of in pieces:
        draws = jnp.exp(jax.random.uniform(jax.random.fold_in(own, position), (shards_of,), jnp.float32, smallest / len(pieces), top_value / len(pieces)))
        gain = gain * jnp.repeat(draws, extent[position] // shards_of).reshape([-1 if axis == position else 1 for axis in range(len(extent))])
    return gain


def normal_values(rng, shape, scale, limit, cuts=(), dtype=jnp.bfloat16):
    array = scale * jax.random.normal(rng, shape, jnp.float32)
    if cuts:
        array = array * shard_levels(rng, shape, cuts, -0.22, 0.18)
    return jnp.clip(array, -limit, limit).astype(dtype)


def noise_with(key, dims, deviation, most, cuts, heavy, held_as=jnp.bfloat16):
    drawn = deviation * jax.random.normal(key, dims, jnp.float32)
    if cuts:
        drawn = drawn * shard_levels(key, dims, cuts, -0.22, 0.18)
    return jnp.clip(with_spikes(drawn, jax.random.fold_in(key, 3), *heavy), -most, most).astype(held_as)


def setup_inputs(seed: int = 0) -> dict:
    key_list = jax.random.split(jax.random.key(seed), 8)
    sec_rhs = normal_values(key_list[0], (RHS, NS * SECTIONS), 1.0, 6.0, ((1, 32),), jnp.float32)
    sec_inverse = draw_sec_inverse(jax.random.fold_in(key_list[7], 71), 0)
    sep_rhs = normal_values(key_list[2], (LEVELS, RHS, NK), 1.0, 6.0, ((2, 8),), jnp.float32)
    sep_inverse = draw_sep_inverse(jax.random.fold_in(key_list[7], 71), 0)
    sep_coupling = normal_values(key_list[4], (LEVELS - 1, NK, NK), NK ** -0.5, 0.1875, ((1, 8),), jnp.float32)
    sec_update = noise_with(key_list[5], (LEVELS, NK, NS * SECTIONS), (NS * SECTIONS) ** -0.5, 0.1875, ((2, 32),), (2, 1, 32, 2.75), jnp.float32)
    link = place_ends((jax.random.randint(key_list[6], (SECTIONS, LEVELS), 0, 4) < 3).astype(jnp.int32), jax.random.fold_in(key_list[6], 1), 0, 1)
    return dict(sec_rhs=sec_rhs, sec_inverse=sec_inverse, sep_rhs=sep_rhs, sep_inverse=sep_inverse, sep_coupling=sep_coupling, sec_update=sec_update, link=link)


def reference(sec_rhs, sec_inverse, sep_rhs, sep_inverse, sep_coupling, sec_update, link):
    highest = lax.Precision.HIGHEST
    link_weights = link.astype(jnp.float32)
    blocks = sec_rhs.reshape(RHS, SECTIONS, NS)
    diag_blocks = sec_inverse.reshape(SECTIONS, NS, NS)
    y_sec = jnp.einsum("rsj,sij->rsi", blocks, diag_blocks, precision=highest)
    y_flat = y_sec.reshape(RHS, SECTIONS * NS)
    y_sep = []
    previous = None
    for level in range(LEVELS):
        scaled = (y_sec * link_weights[:, level][None, :, None]).reshape(RHS, SECTIONS * NS)
        section_sum = jnp.dot(scaled, sec_update[level].T, precision=highest, preferred_element_type=jnp.float32)
        known = sep_rhs[level] - section_sum
        if level > 0:
            known = known - jnp.dot(previous, sep_coupling[level - 1].T, precision=highest, preferred_element_type=jnp.float32)
        previous = jnp.dot(known, sep_inverse[level].T, precision=highest, preferred_element_type=jnp.float32)
        y_sep.append(previous)
    solved = [None] * LEVELS
    for level in range(LEVELS - 1, -1, -1):
        adjusted = y_sep[level]
        if level < LEVELS - 1:
            adjusted = adjusted - jnp.dot(solved[level + 1], sep_coupling[level], precision=highest, preferred_element_type=jnp.float32)
        solved[level] = jnp.dot(adjusted, sep_inverse[level], precision=highest, preferred_element_type=jnp.float32)
    back_sec = y_flat
    for level in range(LEVELS):
        term = jnp.dot(solved[level], sec_update[level], precision=highest, preferred_element_type=jnp.float32)
        term = term.reshape(RHS, SECTIONS, NS) * link_weights[:, level][None, :, None]
        back_sec = back_sec - term.reshape(RHS, SECTIONS * NS)
    back_blocks = back_sec.reshape(RHS, SECTIONS, NS)
    sec_solution = jnp.einsum("rsi,sij->rsj", back_blocks, diag_blocks, precision=highest)
    return sec_solution.reshape(RHS, SECTIONS * NS), jnp.stack(solved)
```

```python
import functools

import jax
import jax.numpy as jnp
from jax import lax
from jax.experimental import pallas as pl
from jax.experimental.pallas import tpu as pltpu
from jax.sharding import PartitionSpec as P

MESH = pl.DeviceIdType.MESH
LAST = (((1,), (1,)), ((), ()))
PLAIN = (((1,), (0,)), ((), ()))
CHUNK = 8


def split(value):
    high = value.astype(jnp.bfloat16)
    low = (value - high.astype(jnp.float32)).astype(jnp.bfloat16)
    return high, low


def dot3(left, right, dims):
    rows = left.shape[0]
    high, low = split(left)
    both = jnp.concatenate([high, low], axis=0)
    first = lax.dot_general(both, right[0], dims, preferred_element_type=jnp.float32)
    second = lax.dot_general(high, right[1], dims, preferred_element_type=jnp.float32)
    return first[:rows] + (first[rows:] + second)


def lanes(ref, start, count):
    return jnp.concatenate([ref[start + i] for i in range(count)], axis=1)


def kernel(
    leaves, rows,
    rhs_h, dinv_h, srhs_h, sinv_h, coup_h, upd_h, link_ref,
    osec_h, osep_h,
    dinv, srhs, sinv, coup, upd,
    rhsb, parts, prow, rs_s, rs_r, fk, fy, bs_s, bs_r, xb, fin_s, fin_r, ob,
    in_sem, leaf_s, leaf_r, row_s, row_r, out_sem,
):
    leaf = lax.axis_index("leaf")
    row = lax.axis_index("row")
    levels = sinv.shape[0]
    q = srhs.shape[1]
    width = fk.shape[3]
    span = min(CHUNK, leaves)
    chunks = leaves // span

    def load(index, src, dst):
        copy = pltpu.make_async_copy(src, dst, in_sem.at[index])
        copy.start()
        return copy

    load_rhs = load(0, rhs_h, rhsb.at[row])
    load_dinv = load(1, dinv_h, dinv)
    load_upd = [load(2 + k, upd_h.at[k], upd.at[k]) for k in range(levels)]
    load_srhs = load(2 + levels, srhs_h.at[:, pl.ds(pl.multiple_of(row * q, q), q), :], srhs)
    load_sinv = load(3 + levels, sinv_h, sinv)
    load_coup = load(4 + levels, coup_h, coup)

    def each_leaf(body):
        def step(d, carry):
            body(lax.rem(leaf + d, leaves))
            return carry
        lax.fori_loop(1, leaves, step, 0)

    def each_row(body):
        for d in range(1, rows):
            body(lax.rem(row + d, rows))

    barrier = pltpu.get_barrier_semaphore()
    each_leaf(lambda p: pl.semaphore_signal(barrier, inc=1, device_id={"leaf": p}, device_id_type=MESH))
    each_row(lambda p: pl.semaphore_signal(barrier, inc=1, device_id={"row": p}, device_id_type=MESH))
    pl.semaphore_wait(barrier, leaves + rows - 2)

    def leaf_send(src_of, dst, index):
        each_leaf(lambda p: pltpu.make_async_remote_copy(
            src_ref=src_of(p), dst_ref=dst, send_sem=leaf_s.at[index], recv_sem=leaf_r.at[index],
            device_id={"leaf": p}, device_id_type=MESH).start())

    def row_send(src_of, dst, index):
        each_row(lambda p: pltpu.make_async_remote_copy(
            src_ref=src_of(p), dst_ref=dst, send_sem=row_s.at[index], recv_sem=row_r.at[index],
            device_id={"row": p}, device_id_type=MESH).start())

    def drain(buf, count, sem):
        ref = buf.at[pl.ds(0, count - 1)]
        pltpu.make_async_copy(ref, ref, sem).wait()

    red_i, fk_i, fy_i = 0, levels, 2 * levels
    bs_i, x_i = 3 * levels - 1, 5 * levels - 2
    part_i, gath_i, fin_i = 1, 1 + levels, 1 + 2 * levels

    row_send(lambda p: rhs_h, rhsb.at[row], 0)
    load_dinv.wait()
    dinv_split = split(dinv[...])
    load_rhs.wait()
    drain(rhsb, rows, row_r.at[0])
    rhs_full = jnp.concatenate([rhsb[i] for i in range(rows)], axis=1)
    y_sec = dot3(rhs_full, dinv_split, LAST)

    weights = [link_ref[0, k].astype(jnp.float32) for k in range(levels)]

    for k in range(levels):
        load_upd[k].wait()
        scaled = y_sec * weights[k]

        def part_step(c, k=k, scaled=scaled):
            cols = pl.ds(c * span * width, span * width)
            value = dot3(scaled, split(upd[k, cols, :]), LAST)
            parts[k, :, :, cols] = value.reshape(rows, q, span * width)

        if chunks == 1:
            part_step(0)
        else:
            pl.loop(0, chunks)(part_step)
        row_send(lambda p: parts.at[k, p], prow.at[k, row], part_i + k)

    def reduce_row(k):
        prow[k, row] = parts[k, row]
        drain(prow.at[k], rows, row_r.at[part_i + k])
        for i in range(leaves):
            cols = pl.ds(i * width, width)
            total = prow[k, 0, :, cols]
            for r in range(1, rows):
                total = total + prow[k, r, :, cols]
            rs_s[k, i] = total
        leaf_send(lambda p: rs_s.at[k, p], rs_r.at[k, leaf], red_i + k)
        rs_r[k, leaf] = rs_s[k, leaf]

    def add_up(ref):
        total = ref[0]
        for i in range(1, leaves):
            total = total + ref[i]
        return total

    def contract(buf, matrix, k, index):
        if chunks == 1:
            prepared = split(matrix[k])
            drain(buf, leaves, leaf_r.at[index])
            return dot3(lanes(buf, 0, span), prepared, LAST)
        drain(buf, leaves, leaf_r.at[index])

        def step(c, total):
            block = split(matrix[k, :, pl.ds(pl.multiple_of(c * span * width, span * width), span * width)])
            return total + dot3(lanes(buf, c * span, span), block, LAST)

        return lax.fori_loop(0, chunks, step, jnp.zeros((q, width), jnp.float32))

    def expand(value, matrix, prepared, k, slot):
        def store(c, block):
            product = dot3(value, block, PLAIN)
            for i in range(span):
                bs_s[slot, c * span + i] = product[:, i * width:(i + 1) * width]

        if chunks == 1:
            store(0, prepared)
        else:
            @pl.loop(0, chunks)
            def _(c):
                store(c, split(matrix[k, :, pl.ds(pl.multiple_of(c * span * width, span * width), span * width)]))
        leaf_send(lambda p: bs_s.at[slot, p], bs_r.at[slot, leaf], bs_i + slot)
        bs_r[slot, leaf] = bs_s[slot, leaf]

    def prepare(matrix, k):
        return split(matrix[k]) if chunks == 1 else None

    def collect(slot):
        drain(bs_r.at[slot], leaves, leaf_r.at[bs_i + slot])
        return add_up(bs_r.at[slot])

    reduce_row(0)
    load_srhs.wait()
    load_sinv.wait()
    load_coup.wait()
    y_leaf = []
    coupled = None
    for k in range(levels):
        drain(rs_r.at[k], leaves, leaf_r.at[red_i + k])
        known = srhs[k] - add_up(rs_r.at[k])
        if k > 0:
            known = known - coupled
        fk[k, leaf] = known
        leaf_send(lambda p: fk.at[k, leaf], fk.at[k, leaf], fk_i + k)
        if k < levels - 1:
            reduce_row(k + 1)
        y_level = contract(fk.at[k], sinv, k, fk_i + k)
        y_leaf.append(y_level)
        if k < levels - 1:
            fy[k, leaf] = y_level
            leaf_send(lambda p: fy.at[k, leaf], fy.at[k, leaf], fy_i + k)
            coupled = contract(fy.at[k], coup, k, fy_i + k)

    outs = []

    def pass_on(k):
        drain(xb.at[k, row], leaves, leaf_r.at[x_i + k])
        row_send(lambda p: xb.at[k, row], xb.at[k, row], gath_i + k)

    def back_term(k):
        def block_of(c):
            start = c * span * width
            if chunks > 1:
                start = pl.multiple_of(start, span * width)
            return split(upd[k, pl.ds(start, span * width), :])

        def gathered(c):
            return jnp.concatenate(
                [lanes(xb.at[k, r], c * span, span) for r in range(rows)], axis=0)

        prepared = block_of(0) if chunks == 1 else None
        drain(xb.at[k], rows, row_r.at[gath_i + k])
        copy = pltpu.make_async_copy(xb.at[k, :, leaf], osep_h.at[k], out_sem.at[k])
        copy.start()
        outs.append(copy)
        if chunks == 1:
            total = dot3(gathered(0), prepared, PLAIN)
        else:
            total = lax.fori_loop(
                0, chunks, lambda c, t: t + dot3(gathered(c), block_of(c), PLAIN),
                jnp.zeros((rows * q, width), jnp.float32))
        return total * weights[k]

    back = y_sec
    slot = 0
    adjusted = y_leaf[levels - 1]
    prepared = prepare(sinv, levels - 1)
    for k in range(levels - 1, -1, -1):
        expand(adjusted, sinv, prepared, k, slot)
        prepared = prepare(coup, k - 1) if k > 0 else None
        if k + 1 < levels:
            pass_on(k + 1)
        solved = collect(slot)
        slot += 1
        if k > 0:
            expand(solved, coup, prepared, k - 1, slot)
            xb[k, row, leaf] = solved
            leaf_send(lambda p: xb.at[k, row, leaf], xb.at[k, row, leaf], x_i + k)
            prepared = prepare(sinv, k - 1)
            if k + 1 < levels:
                back = back - back_term(k + 1)
            adjusted = y_leaf[k - 1] - collect(slot)
            slot += 1
        else:
            xb[k, row, leaf] = solved
            leaf_send(lambda p: xb.at[k, row, leaf], xb.at[k, row, leaf], x_i + k)
    back = back - back_term(1)
    pass_on(0)
    dinv_split = split(dinv[...])
    back = back - back_term(0)
    last = dot3(back, dinv_split, PLAIN)
    for r in range(rows):
        fin_s[r] = last[:, r * width:(r + 1) * width]
    row_send(lambda p: fin_s.at[p], fin_r.at[row], fin_i)
    fin_r[row] = fin_s[row]

    for k in range(levels):
        drain(rs_s.at[k], leaves, leaf_s.at[red_i + k])
        drain(fk.at[k], leaves, leaf_s.at[fk_i + k])
        drain(xb.at[k, row], leaves, leaf_s.at[x_i + k])
        drain(parts.at[k], rows, row_s.at[part_i + k])
        drain(xb.at[k], rows, row_s.at[gath_i + k])
        if k < levels - 1:
            drain(fy.at[k], leaves, leaf_s.at[fy_i + k])
    for s in range(2 * levels - 1):
        drain(bs_s.at[s], leaves, leaf_s.at[bs_i + s])
    drain(rhsb, rows, row_s.at[0])

    drain(fin_r, rows, row_r.at[fin_i])
    total = fin_r[0]
    for r in range(1, rows):
        total = total + fin_r[r]
    ob[...] = total
    copy = pltpu.make_async_copy(ob, osec_h, out_sem.at[levels])
    copy.start()
    outs.append(copy)
    drain(fin_s, rows, row_s.at[fin_i])
    for copy in outs:
        copy.wait()


def per_device(leaves, rows, sec_rhs, sec_inverse, sep_rhs, sep_inverse, sep_coupling, sec_update, link):
    levels, rhs, width = sep_rhs.shape
    full = sep_inverse.shape[2]
    q = rhs // rows
    f32 = jnp.float32
    any_spec = pl.BlockSpec(memory_space=pl.ANY)
    slots = lambda n: pltpu.VMEM((n, leaves, q, width), f32)
    vmem = lambda *shape: pltpu.VMEM(shape, f32)
    leaf_rounds = 6 * levels - 2
    row_rounds = 2 + 2 * levels
    scratch = [
        vmem(*sec_inverse.shape), vmem(levels, q, width), vmem(*sep_inverse.shape),
        vmem(*sep_coupling.shape), vmem(*sec_update.shape),
        vmem(rows, *sec_rhs.shape), vmem(levels, rows, q, full), vmem(levels, rows, q, full),
        slots(levels), slots(levels), slots(levels), slots(levels - 1),
        slots(2 * levels - 1), slots(2 * levels - 1),
        vmem(levels, rows, leaves, q, width),
        vmem(rows, *sec_rhs.shape), vmem(rows, *sec_rhs.shape), vmem(*sec_rhs.shape),
        pltpu.SemaphoreType.DMA((5 + levels,)),
        pltpu.SemaphoreType.DMA((leaf_rounds,)), pltpu.SemaphoreType.DMA((leaf_rounds,)),
        pltpu.SemaphoreType.DMA((row_rounds,)), pltpu.SemaphoreType.DMA((row_rounds,)),
        pltpu.SemaphoreType.DMA((levels + 1,)),
    ]
    sec, sep = pl.pallas_call(
        functools.partial(kernel, leaves, rows),
        out_shape=(
            jax.ShapeDtypeStruct(sec_rhs.shape, f32),
            jax.ShapeDtypeStruct((levels, rows, q, width), f32),
        ),
        in_specs=[any_spec] * 6 + [pl.BlockSpec(memory_space=pltpu.SMEM)],
        out_specs=(any_spec, any_spec),
        scratch_shapes=scratch,
        compiler_params=pltpu.CompilerParams(
            collective_id=0, has_side_effects=True, vmem_limit_bytes=58 * 1024 * 1024),
    )(sec_rhs, sec_inverse, sep_rhs, sep_inverse, sep_coupling, sec_update, link)
    return sec, sep.reshape(levels, rhs, width)


def solution(mesh):
    in_specs = (
        P(None, ("leaf", "row")),
        P(("leaf", "row"), None),
        P(None, None, "leaf"),
        P(None, "leaf", None),
        P(None, "leaf", None),
        P(None, None, ("leaf", "row")),
        P("leaf", None),
    )
    out_specs = (P(None, ("leaf", "row")), P(None, None, "leaf"))
    return jax.shard_map(
        functools.partial(per_device, mesh.shape["leaf"], mesh.shape["row"]),
        mesh=mesh, in_specs=in_specs, out_specs=out_specs, check_vma=False,
    )
```

```python
import functools

import jax
import jax.numpy as jnp
from jax import lax
from jax.experimental import pallas as pl
from jax.experimental.pallas import tpu as pltpu
from jax.sharding import PartitionSpec as P

MESH = pl.DeviceIdType.MESH
LAST = (((1,), (1,)), ((), ()))
PLAIN = (((1,), (0,)), ((), ()))
CHUNK = 8


def split(value):
    high = value.astype(jnp.bfloat16)
    low = (value - high.astype(jnp.float32)).astype(jnp.bfloat16)
    return high, low


def dot3(left, right, dims):
    rows = left.shape[0]
    high, low = split(left)
    both = jnp.concatenate([high, low], axis=0)
    first = lax.dot_general(both, right[0], dims, preferred_element_type=jnp.float32)
    second = lax.dot_general(high, right[1], dims, preferred_element_type=jnp.float32)
    return first[:rows] + (first[rows:] + second)


def lanes(ref, start, count):
    return jnp.concatenate([ref[start + i] for i in range(count)], axis=1)


def kernel(
    leaves, rows,
    rhs_h, dinv_h, srhs_h, sinv_h, coup_h, upd_h, link_ref,
    osec_h, osep_h,
    dinv, srhs, sinv, coup, upd,
    rhsb, parts, prow, rs_s, rs_r, fk, fy, bs_s, bs_r, xb, xs, u0, dfull, base_s, base_r, fin_s, fin_r,
    in_sem, leaf_s, leaf_r, row_s, row_r, out_sem,
):
    leaf = lax.axis_index("leaf")
    row = lax.axis_index("row")
    levels = sinv.shape[0]
    q = srhs.shape[1]
    width = fk.shape[3]
    span = min(CHUNK, leaves)
    chunks = leaves // span

    def load(index, src, dst):
        copy = pltpu.make_async_copy(src, dst, in_sem.at[index])
        copy.start()
        return copy

    load_rhs = load(0, rhs_h, rhsb.at[row])
    load_dinv = load(1, dinv_h, dinv)
    load_upd = [load(2 + k, upd_h.at[k], upd.at[k]) for k in range(levels)]
    load_srhs = load(2 + levels, srhs_h.at[:, pl.ds(pl.multiple_of(row * q, q), q), :], srhs)
    load_sinv = load(3 + levels, sinv_h, sinv)
    load_coup = load(4 + levels, coup_h, coup)

    def each_leaf(body):
        def step(d, carry):
            body(lax.rem(leaf + d, leaves))
            return carry
        lax.fori_loop(1, leaves, step, 0)

    def each_row(body):
        for d in range(1, rows):
            body(lax.rem(row + d, rows))

    barrier = pltpu.get_barrier_semaphore()
    each_leaf(lambda p: pl.semaphore_signal(barrier, inc=1, device_id={"leaf": p}, device_id_type=MESH))
    each_row(lambda p: pl.semaphore_signal(barrier, inc=1, device_id={"row": p}, device_id_type=MESH))
    pl.semaphore_wait(barrier, leaves + rows - 2)

    def leaf_send(src_of, dst, index):
        each_leaf(lambda p: pltpu.make_async_remote_copy(
            src_ref=src_of(p), dst_ref=dst, send_sem=leaf_s.at[index], recv_sem=leaf_r.at[index],
            device_id={"leaf": p}, device_id_type=MESH).start())

    def row_send(src_of, dst, index):
        each_row(lambda p: pltpu.make_async_remote_copy(
            src_ref=src_of(p), dst_ref=dst, send_sem=row_s.at[index], recv_sem=row_r.at[index],
            device_id={"row": p}, device_id_type=MESH).start())

    def drain(buf, count, sem):
        ref = buf.at[pl.ds(0, count - 1)]
        pltpu.make_async_copy(ref, ref, sem).wait()

    red_i, fk_i, fy_i = 0, levels, 2 * levels
    bs_i, x_i = 3 * levels - 1, 5 * levels - 2
    part_i, gath_i, fin_i = 1, 1 + levels, 1 + 2 * levels
    base_i, u0_i, dfull_i = fin_i + 1, fin_i + 2, fin_i + 3

    row_send(lambda p: rhs_h, rhsb.at[row], 0)
    load_dinv.wait()
    dinv_split = split(dinv[...])
    load_rhs.wait()
    drain(rhsb, rows, row_r.at[0])
    rhs_full = jnp.concatenate([rhsb[i] for i in range(rows)], axis=1)
    y_sec = dot3(rhs_full, dinv_split, LAST)

    weights = [link_ref[0, k].astype(jnp.float32) for k in range(levels)]

    for k in range(levels):
        load_upd[k].wait()
        scaled = y_sec * weights[k]

        def part_step(c, k=k, scaled=scaled):
            cols = pl.ds(c * span * width, span * width)
            value = dot3(scaled, split(upd[k, cols, :]), LAST)
            parts[k, :, :, cols] = value.reshape(rows, q, span * width)

        if chunks == 1:
            part_step(0)
        else:
            pl.loop(0, chunks)(part_step)
        row_send(lambda p: parts.at[k, p], prow.at[k, row], part_i + k)

    def reduce_row(k):
        prow[k, row] = parts[k, row]
        drain(prow.at[k], rows, row_r.at[part_i + k])
        for i in range(leaves):
            cols = pl.ds(i * width, width)
            total = prow[k, 0, :, cols]
            for r in range(1, rows):
                total = total + prow[k, r, :, cols]
            rs_s[k, i] = total
        leaf_send(lambda p: rs_s.at[k, p], rs_r.at[k, leaf], red_i + k)
        rs_r[k, leaf] = rs_s[k, leaf]

    def add_up(ref):
        total = ref[0]
        for i in range(1, leaves):
            total = total + ref[i]
        return total

    def contract(buf, matrix, k, index):
        if chunks == 1:
            prepared = split(matrix[k])
            drain(buf, leaves, leaf_r.at[index])
            return dot3(lanes(buf, 0, span), prepared, LAST)
        drain(buf, leaves, leaf_r.at[index])

        def step(c, total):
            block = split(matrix[k, :, pl.ds(pl.multiple_of(c * span * width, span * width), span * width)])
            return total + dot3(lanes(buf, c * span, span), block, LAST)

        return lax.fori_loop(0, chunks, step, jnp.zeros((q, width), jnp.float32))

    def expand(value, matrix, prepared, k, slot):
        def store(c, block):
            product = dot3(value, block, PLAIN)
            for i in range(span):
                bs_s[slot, c * span + i] = product[:, i * width:(i + 1) * width]

        if chunks == 1:
            store(0, prepared)
        else:
            @pl.loop(0, chunks)
            def _(c):
                store(c, split(matrix[k, :, pl.ds(pl.multiple_of(c * span * width, span * width), span * width)]))
        leaf_send(lambda p: bs_s.at[slot, p], bs_r.at[slot, leaf], bs_i + slot)
        bs_r[slot, leaf] = bs_s[slot, leaf]

    def prepare(matrix, k):
        return split(matrix[k]) if chunks == 1 else None

    def collect(slot):
        drain(bs_r.at[slot], leaves, leaf_r.at[bs_i + slot])
        return add_up(bs_r.at[slot])

    reduce_row(0)
    row_send(lambda p: dinv_h, dfull.at[row], dfull_i)
    row_send(lambda p: upd_h.at[0], u0.at[row], u0_i)
    dfull[row] = dinv[...]
    u0[row] = upd[0]
    load_srhs.wait()
    load_sinv.wait()
    load_coup.wait()
    y_leaf = []
    coupled = None
    for k in range(levels):
        drain(rs_r.at[k], leaves, leaf_r.at[red_i + k])
        known = srhs[k] - add_up(rs_r.at[k])
        if k > 0:
            known = known - coupled
        fk[k, leaf] = known
        leaf_send(lambda p: fk.at[k, leaf], fk.at[k, leaf], fk_i + k)
        if k < levels - 1:
            reduce_row(k + 1)
        y_level = contract(fk.at[k], sinv, k, fk_i + k)
        y_leaf.append(y_level)
        if k < levels - 1:
            fy[k, leaf] = y_level
            leaf_send(lambda p: fy.at[k, leaf], fy.at[k, leaf], fy_i + k)
            coupled = contract(fy.at[k], coup, k, fy_i + k)

    outs = []

    def pass_on(k):
        drain(xb.at[k, row], leaves, leaf_r.at[x_i + k])
        row_send(lambda p: xb.at[k, row], xb.at[k, row], gath_i + k)

    def back_term(k):
        def block_of(c):
            start = c * span * width
            if chunks > 1:
                start = pl.multiple_of(start, span * width)
            return split(upd[k, pl.ds(start, span * width), :])

        def gathered(c):
            return jnp.concatenate(
                [lanes(xb.at[k, r], c * span, span) for r in range(rows)], axis=0)

        prepared = block_of(0) if chunks == 1 else None
        drain(xb.at[k], rows, row_r.at[gath_i + k])
        copy = pltpu.make_async_copy(xb.at[k, :, leaf], osep_h.at[k], out_sem.at[k])
        copy.start()
        outs.append(copy)
        if chunks == 1:
            total = dot3(gathered(0), prepared, PLAIN)
        else:
            total = lax.fori_loop(
                0, chunks, lambda c, t: t + dot3(gathered(c), block_of(c), PLAIN),
                jnp.zeros((rows * q, width), jnp.float32))
        return total * weights[k]

    back = y_sec
    slot = 0
    adjusted = y_leaf[levels - 1]
    prepared = prepare(sinv, levels - 1)
    for k in range(levels - 1, -1, -1):
        expand(adjusted, sinv, prepared, k, slot)
        prepared = prepare(coup, k - 1) if k > 0 else None
        if k + 1 < levels:
            pass_on(k + 1)
        solved = collect(slot)
        slot += 1
        if k > 0:
            expand(solved, coup, prepared, k - 1, slot)
            xb[k, row, leaf] = solved
            leaf_send(lambda p: xb.at[k, row, leaf], xb.at[k, row, leaf], x_i + k)
            prepared = prepare(sinv, k - 1)
            if k + 1 < levels:
                back = back - back_term(k + 1)
            adjusted = y_leaf[k - 1] - collect(slot)
            slot += 1
        else:
            xb[k, row, leaf] = solved
            leaf_send(lambda p: xb.at[k, row, leaf], xb.at[k, row, leaf], x_i + k)
    row_send(lambda p: xb.at[0, row, leaf], xs.at[row], gath_i)
    xs[row] = solved
    back = back - back_term(1)
    base_s[...] = back.reshape(rows, q, width)
    row_send(lambda p: base_s.at[p], base_r.at[row], base_i)
    base_r[row] = base_s[row]

    drain(dfull, rows, row_r.at[dfull_i])
    drain(u0, rows, row_r.at[u0_i])

    def section_block(c):
        start = c * span * width
        if chunks > 1:
            start = pl.multiple_of(start, span * width)
        return split(jnp.concatenate(
            [u0[r, pl.ds(start, span * width), :] for r in range(rows)], axis=1))

    prepared = section_block(0) if chunks == 1 else None
    dinv_split = split(jnp.concatenate([dfull[r] for r in range(rows)], axis=0))
    drain(xb.at[0, row], leaves, leaf_r.at[x_i])
    if chunks == 1:
        term = dot3(lanes(xb.at[0, row], 0, span), prepared, PLAIN)
    else:
        term = lax.fori_loop(
            0, chunks,
            lambda c, t: t + dot3(lanes(xb.at[0, row], c * span, span), section_block(c), PLAIN),
            jnp.zeros((q, rows * width), jnp.float32))
    drain(base_r, rows, row_r.at[base_i])
    base = jnp.concatenate([base_r[r] for r in range(rows)], axis=1)
    last = dot3(base - term * weights[0], dinv_split, PLAIN)
    for r in range(rows):
        fin_s[r] = last[:, r * width:(r + 1) * width]
    row_send(lambda p: fin_s.at[p], fin_r.at[row], fin_i)
    fin_r[row] = fin_s[row]
    drain(xs, rows, row_r.at[gath_i])
    copy = pltpu.make_async_copy(xs, osep_h.at[0], out_sem.at[0])
    copy.start()
    outs.append(copy)

    for k in range(levels):
        drain(rs_s.at[k], leaves, leaf_s.at[red_i + k])
        drain(fk.at[k], leaves, leaf_s.at[fk_i + k])
        drain(xb.at[k, row], leaves, leaf_s.at[x_i + k])
        drain(parts.at[k], rows, row_s.at[part_i + k])
        drain(xb.at[k] if k > 0 else xs, rows, row_s.at[gath_i + k])
        if k < levels - 1:
            drain(fy.at[k], leaves, leaf_s.at[fy_i + k])
    for s in range(2 * levels - 1):
        drain(bs_s.at[s], leaves, leaf_s.at[bs_i + s])
    drain(rhsb, rows, row_s.at[0])

    drain(fin_r, rows, row_r.at[fin_i])
    copy = pltpu.make_async_copy(fin_r, osec_h, out_sem.at[levels])
    copy.start()
    outs.append(copy)
    drain(base_s, rows, row_s.at[base_i])
    drain(dfull, rows, row_s.at[dfull_i])
    drain(u0, rows, row_s.at[u0_i])
    drain(fin_s, rows, row_s.at[fin_i])
    for copy in outs:
        copy.wait()


def per_device(leaves, rows, sec_rhs, sec_inverse, sep_rhs, sep_inverse, sep_coupling, sec_update, link):
    levels, rhs, width = sep_rhs.shape
    full = sep_inverse.shape[2]
    q = rhs // rows
    f32 = jnp.float32
    any_spec = pl.BlockSpec(memory_space=pl.ANY)
    slots = lambda n: pltpu.VMEM((n, leaves, q, width), f32)
    vmem = lambda *shape: pltpu.VMEM(shape, f32)
    leaf_rounds = 6 * levels - 2
    row_rounds = 5 + 2 * levels
    scratch = [
        vmem(*sec_inverse.shape), vmem(levels, q, width), vmem(*sep_inverse.shape),
        vmem(*sep_coupling.shape), vmem(*sec_update.shape),
        vmem(rows, *sec_rhs.shape), vmem(levels, rows, q, full), vmem(levels, rows, q, full),
        slots(levels), slots(levels), slots(levels), slots(levels - 1),
        slots(2 * levels - 1), slots(2 * levels - 1),
        vmem(levels, rows, leaves, q, width),
        vmem(rows, q, width), vmem(rows, full, width), vmem(rows, *sec_inverse.shape),
        vmem(rows, q, width), vmem(rows, q, width), vmem(rows, q, width), vmem(rows, q, width),
        pltpu.SemaphoreType.DMA((5 + levels,)),
        pltpu.SemaphoreType.DMA((leaf_rounds,)), pltpu.SemaphoreType.DMA((leaf_rounds,)),
        pltpu.SemaphoreType.DMA((row_rounds,)), pltpu.SemaphoreType.DMA((row_rounds,)),
        pltpu.SemaphoreType.DMA((levels + 1,)),
    ]
    sec, sep = pl.pallas_call(
        functools.partial(kernel, leaves, rows),
        out_shape=(
            jax.ShapeDtypeStruct((rows, q, width), f32),
            jax.ShapeDtypeStruct((levels, rows, q, width), f32),
        ),
        in_specs=[any_spec] * 6 + [pl.BlockSpec(memory_space=pltpu.SMEM)],
        out_specs=(any_spec, any_spec),
        scratch_shapes=scratch,
        compiler_params=pltpu.CompilerParams(
            collective_id=0, has_side_effects=True, vmem_limit_bytes=58 * 1024 * 1024),
    )(sec_rhs, sec_inverse, sep_rhs, sep_inverse, sep_coupling, sec_update, link)
    return sec.reshape(rhs, width), sep.reshape(levels, rhs, width)


def solution(mesh):
    in_specs = (
        P(None, ("leaf", "row")),
        P(("leaf", "row"), None),
        P(None, None, "leaf"),
        P(None, "leaf", None),
        P(None, "leaf", None),
        P(None, None, ("leaf", "row")),
        P("leaf", None),
    )
    out_specs = (P(None, ("leaf", "row")), P(None, None, "leaf"))
    return jax.shard_map(
        functools.partial(per_device, mesh.shape["leaf"], mesh.shape["row"]),
        mesh=mesh, in_specs=in_specs, out_specs=out_specs, check_vma=False,
    )
```
